1024 devices in a mesh: batch: 32 (over y, z_lo), mp: 32 (over x, z_hi, core).
Axes of the slice: x: 8, y: 8, z: 8 (z_hi: 2, z_lo: 4; z = z_hi * 4 + z_lo), core: 2. Of those that a mesh axis runs over, the one named last changes fastest.
Arguments:
- panels: bfloat16 [32, 256, 256, 256], P('mp', None, 'batch'), may hold values from -6 to 6
- cotangent: bfloat16 [32, 256, 256, 256], P('mp', 'batch'), may hold values from -6 to 6
- fm_proj: bfloat16 [256, 16], replicated, may hold values from -0.0234375 to 0.0234375
- mlp_weight: bfloat16 [4096, 16384], P(None, 'mp'), may hold values from -0.09375 to 0.09375
- compress_weight: bfloat16 [192, 256], replicated, may hold values from -0.375 to 0.375
Outputs:
- layer_result_panels: bfloat16 [32, 256, 256, 256], P('mp', 'batch')
- mlp_grad: float32 [4096, 16384], P('batch', 'mp')
The draws below stay inside these ranges and needn't reach their ends.
All inputs are finite; a program needn't handle non-finite values.
Results may differ from the reference program's by a relative error of at most 0.03.
Values may be sent and summed in bfloat16 or wider, within the bound.
No kernel may reach another device: no remote copies, remote signals or barrier semaphores. Data moves between devices by JAX's collectives and lax.ppermute only.
A program may use at most 64 MiB of HBM per device.

```python
import jax
import jax.numpy as jnp
from jax import lax

N = 256
D = 256
K = 16
NF = 64
S_DEV = 8
NL = 192
ROWS = 256
N_BATCH = 32
N_MP = 32


def levels(own_key, shape, split, least, high):
    level, own = 1.0, jax.random.fold_in(own_key, 6)
    for position, blocks in split:
        draws = jnp.exp(jax.random.uniform(jax.random.fold_in(own, position), (blocks,), jnp.float32, least / len(split), high / len(split)))
        level = level * jnp.repeat(draws, shape[position] // blocks).reshape([-1 if axis == position else 1 for axis in range(len(shape))])
    return level


def noise(rng, shape, scale, bound, cuts=(), held_as=jnp.bfloat16):
    factor_of = levels(rng, shape, cuts, -0.22, 0.18) if cuts else 1.0
    values = jax.random.normal(rng, shape, jnp.float32) * scale * factor_of
    return jnp.minimum(jnp.maximum(values, -bound), bound).astype(held_as)


def setup_inputs(seed: int = 0) -> dict:
    streams_of = jax.random.split(jax.random.key(seed), 6)
    return {
        "panels": noise(streams_of[0], (N_MP, ROWS, N, D), 1.0, 6.0, ((0, 32), (2, 32))),
        "cotangent": noise(streams_of[1], (N_MP, ROWS, N, D), 1.0, 6.0, ((0, 32), (1, 32))),
        "fm_proj": noise(streams_of[2], (N, K), (N * D) ** -0.5, 0.0234375),
        "mlp_weight": noise(streams_of[3], (N * K, NF * D), (N * K) ** -0.5, 0.09375, ((1, 32),)),
        "compress_weight": noise(streams_of[4], (NL, N), N ** -0.5, 0.375),
    }


def layer_norm(value_entries):
    mean = lax.optimization_barrier(jnp.mean(value_entries, axis=-1, keepdims=True))
    centred = value_entries - mean
    variance = lax.optimization_barrier(jnp.mean(centred * centred, axis=-1, keepdims=True))
    return centred * lax.rsqrt(variance + 1e-05)

def silu_slope(pre):
    sigma = jax.nn.sigmoid(pre)
    return sigma * (1.0 + pre * (1.0 - sigma))

def reference(panels, cotangent, fm_proj, mlp_weight, compress_weight):
    group = N_MP * S_DEV
    proj_wide = fm_proj.astype(jnp.float32)
    compress_wide_panels = compress_weight.astype(jnp.float32)
    top_precision = lax.Precision.HIGHEST

    def one_group(total, index):
        start = (index * S_DEV).astype(jnp.int32)
        block = lax.dynamic_slice_in_dim(panels, start, S_DEV, 1).reshape(group, N, D)
        grads = lax.dynamic_slice_in_dim(cotangent, start, S_DEV, 1).reshape(group, N, D)
        wide_panels = block.astype(jnp.float32)
        inner = jnp.einsum('snd,nk->sdk', wide_panels, proj_wide, precision=top_precision)
        codes = jnp.einsum('snd,sdk->snk', wide_panels, inner, precision=top_precision).astype(jnp.bfloat16).reshape(group, N * K)
        pre = jnp.dot(codes, mlp_weight, preferred_element_type=jnp.float32)
        fmb = jax.nn.silu(pre).astype(jnp.bfloat16)
        linear_compress_block = jnp.einsum('pm,qmo->qpo', compress_wide_panels, wide_panels, precision=top_precision)
        summed = jnp.concatenate([fmb.reshape(group, NF, D).astype(jnp.float32), linear_compress_block], axis=1) + wide_panels
        normed, pull = jax.vjp(layer_norm, summed)
        grad_summed = pull(grads.astype(jnp.float32))[0]
        grad_fmb = grad_summed[:, :NF].reshape(group, NF * D).astype(jnp.bfloat16)
        grad_pre = (grad_fmb.astype(jnp.float32) * silu_slope(pre)).astype(jnp.bfloat16)
        term = jnp.dot(codes.T, grad_pre, preferred_element_type=jnp.float32).astype(jnp.bfloat16)
        term = lax.optimization_barrier(term).astype(jnp.float32)
        return (total + term, normed.astype(jnp.bfloat16).reshape(N_MP, S_DEV, N, D))
    start_total = jnp.zeros((N * K, NF * D), jnp.float32)
    mlp_grad, outs = lax.scan(one_group, start_total, jnp.arange(N_BATCH, dtype=jnp.int32))
    layer_result_panels = jnp.transpose(outs, (1, 0, 2, 3, 4)).reshape(N_MP, N_BATCH * S_DEV, N, D)
    return (layer_result_panels, mlp_grad)
```

```python
import jax
import jax.numpy as jnp
from jax import lax
from jax.sharding import Mesh
from jax.sharding import PartitionSpec as P

NF = 64
EPS = 1e-05
FINE = (("y", 8), ("pair", 2), ("twin", 2), ("x", 8), ("far", 2), ("core", 2))
BATCH = ("y", "pair", "twin")
MP = ("x", "far", "core")
OTHER = [(0, 1), (1, 0)]


def swap(chunks, axes):
    return lax.all_to_all(chunks, axes, split_axis=0, concat_axis=0, tiled=True)


def normalise(rows):
    mean = jnp.mean(rows, axis=-1, keepdims=True)
    centred = rows - mean
    variance = jnp.mean(centred * centred, axis=-1, keepdims=True)
    inverse = lax.rsqrt(variance + EPS)
    return centred * inverse, inverse


def column_block(codes, weight, rows, grads):
    samples = codes.shape[0]
    own_feats, _, width = rows.shape
    pre = jnp.dot(codes, weight, preferred_element_type=jnp.float32)
    normed, grad_pre = [], []
    for f in range(own_feats):
        v = pre[:, f * width : (f + 1) * width]
        sigma = jax.nn.sigmoid(v)
        fmb = (v * sigma).astype(jnp.bfloat16).astype(jnp.float32)
        y, inverse = normalise(fmb + rows[f].astype(jnp.float32))
        g = grads[f].astype(jnp.float32)
        mean_g = jnp.mean(g, axis=-1, keepdims=True)
        mean_gy = jnp.mean(g * y, axis=-1, keepdims=True)
        grad_fmb = (inverse * (g - mean_g - y * mean_gy)).astype(jnp.bfloat16).astype(jnp.float32)
        normed.append(y.astype(jnp.bfloat16))
        grad_pre.append((grad_fmb * (sigma * (1.0 + v * (1.0 - sigma)))).astype(jnp.bfloat16))
    return jnp.stack(normed), jnp.concatenate(grad_pre, axis=1)


def shards(panels, cotangent, fm_proj, mlp_weight, compress_weight):
    blocks = lax.axis_size(BATCH)
    owners = lax.axis_size(MP)
    peers = owners // 2
    core = lax.axis_index("core")
    twin = lax.axis_index("twin")
    group, feats_dev, width = panels.shape[1:]
    samples = group // blocks
    feats = feats_dev * blocks
    rank = fm_proj.shape[1]
    own_feats = NF // owners
    half = peers * samples
    code_cols = feats * rank
    code_blocks = code_cols // width
    lanes = width // 2

    owned = swap(panels.reshape(blocks, samples, feats_dev, width), BATCH)
    wide = owned.transpose(1, 0, 2, 3).reshape(samples, feats, width)
    inner = jnp.einsum("snd,nk->sdk", wide, fm_proj, preferred_element_type=jnp.float32)
    codes = jnp.einsum(
        "snd,sdk->snk", wide.astype(jnp.float32), inner, precision=lax.Precision.HIGHEST
    )
    codes = codes.astype(jnp.bfloat16).reshape(samples, code_blocks, width).transpose(1, 0, 2)

    def by_peer(rows):
        rows = rows.reshape(samples, peers, 2, own_feats, width).transpose(1, 2, 3, 0, 4)
        return jnp.where(core == 0, rows, rows[:, ::-1])

    head_rows = by_peer(wide[:, :NF])
    head_grads = by_peer(cotangent[0, :, :NF])
    parcel = jnp.concatenate(
        [
            jnp.broadcast_to(codes, (peers, *codes.shape)),
            head_rows[:, 0],
            head_grads[:, 0],
            head_rows[:, 1],
            head_grads[:, 1],
        ],
        axis=1,
    )
    parcel = swap(parcel, ("x", "far"))
    ends = [code_blocks + own_feats * i for i in range(5)]

    def rows_of(first):
        return parcel[:, ends[first] : ends[first + 1]]

    mine = (parcel[:, :code_blocks], rows_of(0), rows_of(1))
    other = lax.ppermute(
        jnp.concatenate([mine[0], rows_of(2), rows_of(3)], axis=1), "core", OTHER
    )
    other = (other[:, :code_blocks], other[:, ends[0] : ends[1]], other[:, ends[1] : ends[2]])

    def lane_half(blocked, which):
        return jnp.where(which == 0, blocked[..., :lanes], blocked[..., lanes:])

    sent = lane_half(mine[0], 1 - twin)
    twin_mine = lax.ppermute(sent, "twin", OTHER)
    twin_other = lax.ppermute(twin_mine, "core", OTHER)

    normed, grad_pre = [], []
    for blocked, rows, grads in (mine, other):
        flat = blocked.transpose(0, 2, 1, 3).reshape(half, code_cols)
        tall = [a.transpose(1, 0, 2, 3).reshape(own_feats, half, width) for a in (rows, grads)]
        y, g = column_block(flat, mlp_weight, *tall)
        normed.append(y)
        grad_pre.append(g)
    grad_pre = jnp.concatenate(grad_pre, axis=0)
    twin_grad = lax.ppermute(grad_pre, "twin", OTHER)

    def columns(blocked):
        return blocked.transpose(0, 2, 1, 3).reshape(half, code_blocks * lanes)

    left = jnp.concatenate(
        [columns(a) for a in (lane_half(mine[0], twin), lane_half(other[0], twin), twin_mine, twin_other)]
    )
    right = jnp.concatenate([grad_pre, twin_grad])
    term = jnp.einsum("sc,so->co", left, right, preferred_element_type=jnp.float32)
    term = term.astype(jnp.bfloat16).reshape(code_blocks, lanes, -1)
    mlp_grad = jnp.sum(swap(term, ("y", "pair")).astype(jnp.float32), axis=0)

    back = jnp.stack(normed).reshape(2, own_feats, peers, samples, width)
    back = jnp.where(core == 0, back, back[::-1]).transpose(2, 0, 1, 3, 4)
    back = swap(back.reshape(owners, own_feats, samples, width), MP)
    head = back.transpose(2, 0, 1, 3).reshape(samples, NF, width)
    lcb = jnp.einsum("pm,qmo->qpo", compress_weight, wide, preferred_element_type=jnp.float32)
    tail, _ = normalise(lcb + wide[:, NF:].astype(jnp.float32))
    result = jnp.concatenate([head, tail.astype(jnp.bfloat16)], axis=1)
    return result[None], mlp_grad


def solution(mesh):
    fine = Mesh(mesh.devices.reshape([n for _, n in FINE]), [name for name, _ in FINE])
    in_specs = (P(MP, None, BATCH, None), P(MP, BATCH, None, None), P(), P(None, MP), P())
    out_specs = (P(MP, BATCH, None, None), P(BATCH, MP))
    return jax.shard_map(shards, mesh=fine, in_specs=in_specs, out_specs=out_specs, check_vma=False)
```

```python
import jax
import jax.numpy as jnp
from jax import lax
from jax.sharding import Mesh
from jax.sharding import PartitionSpec as P

NF = 64
EPS = 1e-05
FINE = (("yh", 4), ("yl", 2), ("pair", 2), ("twin", 2), ("x", 8), ("far", 2), ("core", 2))
BATCH = ("yh", "yl", "pair", "twin")
MP = ("x", "far", "core")


def swap(chunks, axes):
    return lax.all_to_all(chunks, axes, split_axis=0, concat_axis=0, tiled=True)


def across(array, axis, distance=1):
    count = lax.axis_size(axis)
    return lax.ppermute(array, axis, [(i, i ^ distance) for i in range(count)])


def after(array, *others):
    return lax.optimization_barrier((array, *others))[0]


def pick(array, axis, index):
    return jnp.where(
        index == 0, lax.index_in_dim(array, 0, axis, False), lax.index_in_dim(array, 1, axis, False)
    )


def ordered(own, other, axis, index):
    return jnp.where(index == 0, jnp.stack([own, other], axis), jnp.stack([other, own], axis))


def cube_swap(buffer, axis, index, name, distance=1):
    sent = pick(buffer, axis, 1 - index)
    received = across(sent.reshape(-1, sent.shape[-1]), name, distance).reshape(sent.shape)
    return ordered(pick(buffer, axis, index), received, axis, index)


def normalise(rows):
    mean = jnp.mean(rows, axis=-1, keepdims=True)
    centred = rows - mean
    variance = jnp.mean(centred * centred, axis=-1, keepdims=True)
    inverse = lax.rsqrt(variance + EPS)
    return centred * inverse, inverse


def column_block(codes, weight, rows, grads):
    own_feats, _, width = rows.shape
    pre = jnp.dot(codes, weight, preferred_element_type=jnp.float32)
    normed, grad_pre = [], []
    for f in range(own_feats):
        v = pre[:, f * width : (f + 1) * width]
        sigma = jax.nn.sigmoid(v)
        fmb = (v * sigma).astype(jnp.bfloat16).astype(jnp.float32)
        y, inverse = normalise(fmb + rows[f].astype(jnp.float32))
        g = grads[f].astype(jnp.float32)
        mean_g = jnp.mean(g, axis=-1, keepdims=True)
        mean_gy = jnp.mean(g * y, axis=-1, keepdims=True)
        grad_fmb = (inverse * (g - mean_g - y * mean_gy)).astype(jnp.bfloat16).astype(jnp.float32)
        normed.append(y.astype(jnp.bfloat16))
        grad_pre.append((grad_fmb * (sigma * (1.0 + v * (1.0 - sigma)))).astype(jnp.bfloat16))
    return jnp.stack(normed), jnp.concatenate(grad_pre, axis=1)


def shards(panels, cotangent, fm_proj, mlp_weight, compress_weight):
    blocks = lax.axis_size(BATCH)
    owners = lax.axis_size(MP)
    peers = owners // 2
    lines = lax.axis_size("x")
    core, twin, yl, x = (lax.axis_index(name) for name in ("core", "twin", "yl", "x"))
    far = lax.axis_index("far")
    group, feats_dev, width = panels.shape[1:]
    samples = group // blocks
    feats = feats_dev * blocks
    rank = fm_proj.shape[1]
    own_feats = NF // owners
    half = peers * samples
    code_cols = feats * rank
    code_blocks = code_cols // width
    lanes = width // 2

    owned = swap(panels.reshape(blocks, samples, feats_dev, width), BATCH)
    wide = owned.transpose(1, 0, 2, 3).reshape(samples, feats, width)
    inner = jnp.einsum("snd,nk->sdk", wide, fm_proj, preferred_element_type=jnp.float32)
    codes = jnp.einsum(
        "snd,sdk->snk", wide.astype(jnp.float32), inner, precision=lax.Precision.HIGHEST
    )
    codes = codes.astype(jnp.bfloat16).reshape(samples, code_blocks, width).transpose(1, 0, 2)

    def gathered(block):
        wide_block = block.reshape(-1, block.shape[-1])
        pair = ordered(wide_block, across(wide_block, "far"), 0, far)
        pair = lax.all_gather(pair.reshape(-1, pair.shape[-1]), "x", axis=0, tiled=True)
        return pair.reshape(peers, *block.shape)

    def twin_lanes(blocked, which):
        return pick(blocked.reshape(*blocked.shape[:-1], 2, lanes), -2, which)

    def yl_blocks(blocked, which):
        lead = blocked.shape[: blocked.ndim - 3]
        split = blocked.reshape(*lead, code_blocks // 4, 2, 2, *blocked.shape[-2:])
        return pick(split, len(lead) + 1, which).reshape(*lead, code_blocks // 2, *blocked.shape[-2:])

    own = twin_lanes(codes, twin)
    from_twin = across(twin_lanes(codes, 1 - twin), "twin")
    two = jnp.stack([own, from_twin])
    from_near = across(yl_blocks(two, 1 - yl).reshape(-1, lanes), "yl")
    own_two = yl_blocks(two, yl)
    four = jnp.concatenate([own_two, from_near.reshape(own_two.shape)])

    def by_owner(rows):
        return rows.reshape(samples, owners, own_feats, width).transpose(1, 2, 0, 3)

    heads = jnp.concatenate([by_owner(wide[:, :NF]), by_owner(cotangent[0, :, :NF])], axis=1)
    heads = swap(after(heads.reshape(owners, -1, width), from_twin), MP)
    heads = heads.reshape(peers, 2, 2, own_feats, samples, width).transpose(1, 2, 3, 0, 4, 5)
    heads = heads.reshape(2, 2, own_feats, half, width)

    mine = gathered(codes)
    other = across(mine.reshape(-1, width), "core").reshape(mine.shape)
    left_mine = gathered(after(four, mine))

    normed, grad_pre = [], []
    for codes_half, index in ((mine, core), (other, 1 - core)):
        flat = codes_half.transpose(0, 2, 1, 3).reshape(half, code_cols)
        y, g = column_block(flat, mlp_weight, *pick(heads, 0, index))
        normed.append(y)
        grad_pre.append(g)
    grad_pre = jnp.concatenate(grad_pre, axis=0)
    twin_grads = across(grad_pre, "twin")
    near_grads = jnp.concatenate([across(grad_pre, "yl"), across(twin_grads, "yl")], axis=0)
    grads = jnp.concatenate([grad_pre, twin_grads], axis=0)
    left_mine = after(left_mine, twin_grads)
    left_other = across(left_mine.reshape(-1, lanes), "core").reshape(left_mine.shape)

    def product(neighbour, right):
        flat = [
            part[:, i].transpose(0, 2, 1, 3).reshape(half, code_blocks // 2 * lanes)
            for i in (neighbour, neighbour + 1)
            for part in (left_mine, left_other)
        ]
        left = jnp.concatenate(flat, axis=0)
        return jnp.einsum("sc,so->co", left, right, preferred_element_type=jnp.float32)

    term = product(0, grads) + product(2, near_grads)
    term = term.astype(jnp.bfloat16).reshape(code_blocks // 2, lanes, -1)
    mlp_grad = jnp.sum(swap(term, ("yh", "pair")).astype(jnp.float32), axis=0)

    back = jnp.stack(normed).reshape(2, own_feats, lines, 2, samples, width)
    back = after(back, twin_grads)
    back = ordered(back[0], back[1], 0, core).transpose(2, 3, 0, 1, 4, 5)
    back = cube_swap(back, 2, core, "core")
    back = cube_swap(back, 1, far, "far")
    back = after(back, term)
    for step in range(lines.bit_length() - 1):
        distance = 1 << step
        split = back.reshape(lines // distance // 2, 2, distance, *back.shape[1:])
        bit = (x >> step) & 1
        back = cube_swap(split, 1, bit, "x", distance).reshape(back.shape)
    head = back.transpose(4, 0, 1, 2, 3, 5).reshape(samples, NF, width)

    lcb = jnp.einsum("pm,qmo->qpo", compress_weight, wide, preferred_element_type=jnp.float32)
    tail, _ = normalise(lcb + wide[:, NF:].astype(jnp.float32))
    result = jnp.concatenate([head, tail.astype(jnp.bfloat16)], axis=1)
    return result[None], mlp_grad


def solution(mesh):
    fine = Mesh(mesh.devices.reshape([n for _, n in FINE]), [name for name, _ in FINE])
    in_specs = (P(MP, None, BATCH, None), P(MP, BATCH, None, None), P(), P(None, MP), P())
    out_specs = (P(MP, BATCH, None, None), P(BATCH, MP))
    return jax.shard_map(shards, mesh=fine, in_specs=in_specs, out_specs=out_specs, check_vma=False)
```

```python
import jax
import jax.numpy as jnp
from jax import lax
from jax.sharding import Mesh
from jax.sharding import PartitionSpec as P

NF = 64
EPS = 1e-05
FINE = (("yh", 4), ("yl", 2), ("pair", 2), ("twin", 2), ("x", 8), ("far", 2), ("core", 2))
BATCH = ("yh", "yl", "pair", "twin")
MP = ("x", "far", "core")


def swap(chunks, axes):
    return lax.all_to_all(chunks, axes, split_axis=0, concat_axis=0, tiled=True)


def across(array, axis, distance=1):
    count = lax.axis_size(axis)
    return lax.ppermute(array, axis, [(i, i ^ distance) for i in range(count)])


def after(array, *others):
    return lax.optimization_barrier((array, *others))[0]


def pick(array, axis, index):
    return jnp.where(
        index == 0, lax.index_in_dim(array, 0, axis, False), lax.index_in_dim(array, 1, axis, False)
    )


def ordered(own, other, axis, index):
    return jnp.where(index == 0, jnp.stack([own, other], axis), jnp.stack([other, own], axis))


def cube_swap(buffer, axis, index, name, distance=1):
    sent = pick(buffer, axis, 1 - index)
    received = across(sent.reshape(-1, sent.shape[-1]), name, distance).reshape(sent.shape)
    return ordered(pick(buffer, axis, index), received, axis, index)


def normalise(rows):
    mean = jnp.mean(rows, axis=-1, keepdims=True)
    centred = rows - mean
    variance = jnp.mean(centred * centred, axis=-1, keepdims=True)
    inverse = lax.rsqrt(variance + EPS)
    return centred * inverse, inverse


def column_block(codes, weight, rows, grads):
    own_feats, _, width = rows.shape
    pre = jnp.dot(codes, weight, preferred_element_type=jnp.float32)
    normed, grad_pre = [], []
    for f in range(own_feats):
        v = pre[:, f * width : (f + 1) * width]
        sigma = jax.nn.sigmoid(v)
        fmb = (v * sigma).astype(jnp.bfloat16).astype(jnp.float32)
        y, inverse = normalise(fmb + rows[f].astype(jnp.float32))
        g = grads[f].astype(jnp.float32)
        mean_g = jnp.mean(g, axis=-1, keepdims=True)
        mean_gy = jnp.mean(g * y, axis=-1, keepdims=True)
        grad_fmb = (inverse * (g - mean_g - y * mean_gy)).astype(jnp.bfloat16).astype(jnp.float32)
        normed.append(y.astype(jnp.bfloat16))
        grad_pre.append((grad_fmb * (sigma * (1.0 + v * (1.0 - sigma)))).astype(jnp.bfloat16))
    return jnp.stack(normed), jnp.concatenate(grad_pre, axis=1)


def shards(panels, cotangent, fm_proj, mlp_weight, compress_weight):
    blocks = lax.axis_size(BATCH)
    owners = lax.axis_size(MP)
    peers = owners // 2
    lines = lax.axis_size("x")
    core, twin, yl, x = (lax.axis_index(name) for name in ("core", "twin", "yl", "x"))
    far = lax.axis_index("far")
    group, feats_dev, width = panels.shape[1:]
    samples = group // blocks
    feats = feats_dev * blocks
    rank = fm_proj.shape[1]
    own_feats = NF // owners
    half = peers * samples
    code_cols = feats * rank
    code_blocks = code_cols // width
    lanes = width // 2

    owned = swap(panels.reshape(blocks, samples, feats_dev, width), BATCH)
    wide = owned.transpose(1, 0, 2, 3).reshape(samples, feats, width)
    inner = jnp.einsum("snd,nk->sdk", wide, fm_proj, preferred_element_type=jnp.float32)
    codes = jnp.einsum(
        "snd,sdk->snk", wide.astype(jnp.float32), inner, precision=lax.Precision.HIGHEST
    )
    codes = codes.astype(jnp.bfloat16).reshape(samples, code_blocks, width).transpose(1, 0, 2)

    def twin_lanes(blocked, which):
        return pick(blocked.reshape(*blocked.shape[:-1], 2, lanes), -2, which)

    def yl_blocks(blocked, which):
        lead = blocked.shape[: blocked.ndim - 3]
        split = blocked.reshape(*lead, code_blocks // 4, 2, 2, *blocked.shape[-2:])
        return pick(split, len(lead) + 1, which).reshape(*lead, code_blocks // 2, *blocked.shape[-2:])

    def x_swap(buffer, step):
        distance = 1 << step
        split = buffer.reshape(lines // distance // 2, 2, distance, *buffer.shape[1:])
        return cube_swap(split, 1, (x >> step) & 1, "x", distance).reshape(buffer.shape)

    def by_owner(rows):
        rows = rows.reshape(samples, owners, own_feats, width).transpose(1, 2, 0, 3)
        return rows.reshape(lines, 2, 2, own_feats, samples, width)

    steps = range(lines.bit_length() - 1)
    head_grads = x_swap(by_owner(cotangent[0, :, :NF]), 0)

    code_rows = code_blocks * samples
    head_rows = own_feats * samples
    parcel = jnp.broadcast_to(codes.reshape(-1, width), (peers, code_rows, width))
    heads = by_owner(wide[:, :NF])
    heads = jnp.where(core == 0, heads, heads[:, :, ::-1]).reshape(peers, 2 * head_rows, width)
    parcel = jnp.concatenate([parcel, heads], axis=1)
    parcel_mine = swap(parcel, ("x", "far"))
    parcel_other = across(parcel_mine.reshape(-1, width), "core").reshape(parcel_mine.shape)
    mine, other = (
        p[:, :code_rows].reshape(peers, code_blocks, samples, width)
        for p in (parcel_mine, parcel_other)
    )
    rows_mine = parcel_mine[:, code_rows : code_rows + head_rows]
    rows_other = parcel_other[:, code_rows + head_rows :]

    head_grads = after(head_grads, parcel)
    for step in steps[1:]:
        head_grads = x_swap(head_grads, step)
    head_grads = cube_swap(head_grads, 1, far, "far").reshape(peers, 2, head_rows, width)
    grads_mine = pick(head_grads, 1, core)
    grads_other = after(pick(head_grads, 1, 1 - core), parcel_mine)
    grads_other = across(grads_other.reshape(-1, width), "core").reshape(grads_mine.shape)

    def tall(rows):
        rows = rows.reshape(peers, own_feats, samples, width).transpose(1, 0, 2, 3)
        return rows.reshape(own_feats, half, width)

    def exchanged(blocked, axis):
        return across(blocked.reshape(-1, lanes), axis).reshape(blocked.shape)

    own_codes = twin_lanes(mine, twin)
    twin_codes = exchanged(twin_lanes(mine, 1 - twin), "twin")
    near_codes = exchanged(yl_blocks(own_codes, 1 - yl), "yl")

    normed, grad_pre = [], []
    for part, rows, cots in ((mine, rows_mine, grads_mine), (other, rows_other, grads_other)):
        flat = part.transpose(0, 2, 1, 3).reshape(half, code_cols)
        y, g = column_block(flat, mlp_weight, tall(rows), tall(cots))
        normed.append(y)
        grad_pre.append(g)
    grad_pre = jnp.concatenate(grad_pre, axis=0)
    twin_grads = across(grad_pre, "twin")
    near_grads = jnp.concatenate([across(grad_pre, "yl"), across(twin_grads, "yl")], axis=0)
    grads = jnp.concatenate([grad_pre, twin_grads], axis=0)

    twin_codes = after(twin_codes, grad_pre)
    near_twin = exchanged(yl_blocks(twin_codes, 1 - yl), "yl")
    others = jnp.stack([yl_blocks(twin_codes, yl), near_codes, near_twin])
    left_mine = (yl_blocks(own_codes, yl), *others)
    left_other = (yl_blocks(twin_lanes(other, twin), yl), *exchanged(others, "core"))

    def product(neighbour, right):
        flat = [
            part[i].transpose(0, 2, 1, 3).reshape(half, code_blocks // 2 * lanes)
            for i in (neighbour, neighbour + 1)
            for part in (left_mine, left_other)
        ]
        left = jnp.concatenate(flat, axis=0)
        return jnp.einsum("sc,so->co", left, right, preferred_element_type=jnp.float32)

    term = product(0, grads) + product(2, near_grads)
    term = term.astype(jnp.bfloat16).reshape(code_blocks // 2, lanes, -1)
    mlp_grad = jnp.sum(swap(term, ("yh", "pair")).astype(jnp.float32), axis=0)

    back = jnp.stack(normed).reshape(2, own_feats, lines, 2, samples, width)
    back = after(back, twin_grads)
    back = ordered(back[0], back[1], 0, core).transpose(2, 3, 0, 1, 4, 5)
    back = cube_swap(back, 2, core, "core")
    back = cube_swap(back, 1, far, "far")
    back = after(back, term)
    for step in steps:
        back = x_swap(back, step)
    head = back.transpose(4, 0, 1, 2, 3, 5).reshape(samples, NF, width)

    lcb = jnp.einsum("pm,qmo->qpo", compress_weight, wide, preferred_element_type=jnp.float32)
    tail, _ = normalise(lcb + wide[:, NF:].astype(jnp.float32))
    result = jnp.concatenate([head, tail.astype(jnp.bfloat16)], axis=1)
    return result[None], mlp_grad


def solution(mesh):
    fine = Mesh(mesh.devices.reshape([n for _, n in FINE]), [name for name, _ in FINE])
    in_specs = (P(MP, None, BATCH, None), P(MP, BATCH, None, None), P(), P(None, MP), P())
    out_specs = (P(MP, BATCH, None, None), P(BATCH, MP))
    return jax.shard_map(shards, mesh=fine, in_specs=in_specs, out_specs=out_specs, check_vma=False)
```

```python
import jax
import jax.numpy as jnp
from jax import lax
from jax.sharding import Mesh
from jax.sharding import PartitionSpec as P

NF = 64
EPS = 1e-05
FINE = (("yh", 4), ("yl", 2), ("pair", 2), ("twin", 2), ("x", 8), ("far", 2), ("core", 2))
BATCH = ("yh", "yl", "pair", "twin")
MP = ("x", "far", "core")


def swap(chunks, axes):
    return lax.all_to_all(chunks, axes, split_axis=0, concat_axis=0, tiled=True)


def across(array, axis, distance=1):
    count = lax.axis_size(axis)
    return lax.ppermute(array, axis, [(i, i ^ distance) for i in range(count)])


def after(array, *others):
    return lax.optimization_barrier((array, *others))[0]


def pick(array, axis, index):
    return jnp.where(
        index == 0, lax.index_in_dim(array, 0, axis, False), lax.index_in_dim(array, 1, axis, False)
    )


def ordered(own, other, axis, index):
    return jnp.where(index == 0, jnp.stack([own, other], axis), jnp.stack([other, own], axis))


def cube_swap(buffer, axis, index, name, distance=1):
    sent = pick(buffer, axis, 1 - index)
    received = across(sent.reshape(-1, sent.shape[-1]), name, distance).reshape(sent.shape)
    return ordered(pick(buffer, axis, index), received, axis, index)


def normalise(rows):
    mean = jnp.mean(rows, axis=-1, keepdims=True)
    centred = rows - mean
    variance = jnp.mean(centred * centred, axis=-1, keepdims=True)
    inverse = lax.rsqrt(variance + EPS)
    return centred * inverse, inverse


def column_block(codes, weight, rows, grads):
    own_feats, _, width = rows.shape
    pre = jnp.dot(codes, weight, preferred_element_type=jnp.float32)
    normed, grad_pre = [], []
    for f in range(own_feats):
        v = pre[:, f * width : (f + 1) * width]
        sigma = jax.nn.sigmoid(v)
        fmb = (v * sigma).astype(jnp.bfloat16).astype(jnp.float32)
        y, inverse = normalise(fmb + rows[f].astype(jnp.float32))
        g = grads[f].astype(jnp.float32)
        mean_g = jnp.mean(g, axis=-1, keepdims=True)
        mean_gy = jnp.mean(g * y, axis=-1, keepdims=True)
        grad_fmb = (inverse * (g - mean_g - y * mean_gy)).astype(jnp.bfloat16).astype(jnp.float32)
        normed.append(y.astype(jnp.bfloat16))
        grad_pre.append((grad_fmb * (sigma * (1.0 + v * (1.0 - sigma)))).astype(jnp.bfloat16))
    return jnp.stack(normed), jnp.concatenate(grad_pre, axis=1)


def shards(panels, cotangent, fm_proj, mlp_weight, compress_weight):
    blocks = lax.axis_size(BATCH)
    owners = lax.axis_size(MP)
    peers = owners // 2
    lines = lax.axis_size("x")
    core, far, x = (lax.axis_index(name) for name in ("core", "far", "x"))
    group, feats_dev, width = panels.shape[1:]
    samples = group // blocks
    feats = feats_dev * blocks
    rank = fm_proj.shape[1]
    own_feats = NF // owners
    half = peers * samples
    code_cols = feats * rank
    code_blocks = code_cols // width
    lanes = width // 2

    owned = swap(panels.reshape(blocks, samples, feats_dev, width), BATCH)
    wide = owned.transpose(1, 0, 2, 3).reshape(samples, feats, width)
    inner = jnp.einsum("snd,nk->sdk", wide, fm_proj, preferred_element_type=jnp.float32)
    codes = jnp.einsum(
        "snd,sdk->snk", wide.astype(jnp.float32), inner, precision=lax.Precision.HIGHEST
    )
    codes = codes.astype(jnp.bfloat16).reshape(samples, code_blocks, width).transpose(1, 0, 2)

    def x_swap(buffer, step):
        distance = 1 << step
        split = buffer.reshape(lines // distance // 2, 2, distance, *buffer.shape[1:])
        return cube_swap(split, 1, (x >> step) & 1, "x", distance).reshape(buffer.shape)

    def by_owner(rows):
        rows = rows.reshape(samples, owners, own_feats, width).transpose(1, 2, 0, 3)
        return rows.reshape(lines, 2, 2, own_feats, samples, width)

    code_rows = code_blocks * samples
    head_rows = own_feats * samples
    heads = [by_owner(wide[:, :NF]), by_owner(cotangent[0, :, :NF])]
    heads = [h.reshape(peers, 2, head_rows, width) for h in heads]
    heads = [jnp.where(core == 0, h, h[:, ::-1]).reshape(peers, 2 * head_rows, width) for h in heads]
    parcel = jnp.broadcast_to(codes.reshape(-1, width), (peers, code_rows, width))
    parcel = jnp.concatenate([parcel, *heads], axis=1)
    parcel_mine = swap(parcel, ("x", "far"))
    parcel_other = across(parcel_mine.reshape(-1, width), "core").reshape(parcel_mine.shape)
    mine, other = (
        p[:, :code_rows].reshape(peers, code_blocks, samples, width)
        for p in (parcel_mine, parcel_other)
    )

    def heads_of(part, which):
        starts = [code_rows + which * head_rows, code_rows + (2 + which) * head_rows]
        return [tall(part[:, i : i + head_rows]) for i in starts]

    def tall(rows):
        rows = rows.reshape(peers, own_feats, samples, width).transpose(1, 0, 2, 3)
        return rows.reshape(own_feats, half, width)

    near_blocks = code_blocks // 2
    left_mine = mine.reshape(peers, code_blocks // 4, 2, 2, samples, 2, lanes)
    left_mine = left_mine.transpose(2, 5, 0, 1, 3, 4, 6).reshape(4, -1, lanes)
    left_mine = swap(left_mine, ("yl", "twin"))
    left_other = across(left_mine.reshape(-1, lanes), "core")

    def columns(left):
        left = left.reshape(4 * peers, near_blocks, samples, lanes).transpose(0, 2, 1, 3)
        return left.reshape(4 * half, near_blocks * lanes)

    normed, grad_pre = [], []
    for part, blocked, which in ((parcel_mine, mine, 0), (parcel_other, other, 1)):
        flat = blocked.transpose(0, 2, 1, 3).reshape(half, code_cols)
        y, g = column_block(flat, mlp_weight, *heads_of(part, which))
        normed.append(y)
        grad_pre.append(g)
    grad_pre = jnp.concatenate(grad_pre, axis=0)
    near_grads = jnp.broadcast_to(grad_pre, (4, *grad_pre.shape))
    near_grads = after(near_grads, left_mine)
    back = after(jnp.stack(normed), near_grads)
    near_grads = swap(near_grads, ("yl", "twin")).reshape(4, 2, half, -1)

    def product(left, right):
        right = right.reshape(4 * half, -1)
        return jnp.einsum("sc,so->co", columns(left), right, preferred_element_type=jnp.float32)

    term = product(left_mine, near_grads[:, 0]) + product(left_other, near_grads[:, 1])
    term = term.astype(jnp.bfloat16).reshape(code_blocks // 2, lanes, -1)
    mlp_grad = jnp.sum(swap(term, ("yh", "pair")).astype(jnp.float32), axis=0)

    steps = range(lines.bit_length() - 1)
    back = back.reshape(2, own_feats, lines, 2, samples, width)
    back = ordered(back[0], back[1], 0, core).transpose(2, 3, 0, 1, 4, 5)
    back = cube_swap(back, 2, core, "core")
    back = cube_swap(back, 1, far, "far")
    back = after(back, term)
    for step in steps:
        back = x_swap(back, step)
    head = back.transpose(4, 0, 1, 2, 3, 5).reshape(samples, NF, width)

    lcb = jnp.einsum("pm,qmo->qpo", compress_weight, wide, preferred_element_type=jnp.float32)
    tail, _ = normalise(lcb + wide[:, NF:].astype(jnp.float32))
    result = jnp.concatenate([head, tail.astype(jnp.bfloat16)], axis=1)
    return result[None], mlp_grad


def solution(mesh):
    fine = Mesh(mesh.devices.reshape([n for _, n in FINE]), [name for name, _ in FINE])
    in_specs = (P(MP, None, BATCH, None), P(MP, BATCH, None, None), P(), P(None, MP), P())
    out_specs = (P(MP, BATCH, None, None), P(BATCH, MP))
    return jax.shard_map(shards, mesh=fine, in_specs=in_specs, out_specs=out_specs, check_vma=False)
```

```python
import jax
import jax.numpy as jnp
from jax import lax
from jax.sharding import Mesh
from jax.sharding import PartitionSpec as P

NF = 64
EPS = 1e-05
FINE = (("yh", 4), ("yl", 2), ("pair", 2), ("twin", 2), ("x", 8), ("far", 2), ("core", 2))
BATCH = ("yh", "yl", "pair", "twin")
MP = ("x", "far", "core")


def swap(chunks, axes):
    return lax.all_to_all(chunks, axes, split_axis=0, concat_axis=0, tiled=True)


def across(array, axis, distance=1):
    count = lax.axis_size(axis)
    return lax.ppermute(array, axis, [(i, i ^ distance) for i in range(count)])


def after(array, *others):
    return lax.optimization_barrier((array, *others))[0]


def pick(array, axis, index):
    return jnp.where(
        index == 0, lax.index_in_dim(array, 0, axis, False), lax.index_in_dim(array, 1, axis, False)
    )


def ordered(own, other, axis, index):
    return jnp.where(index == 0, jnp.stack([own, other], axis), jnp.stack([other, own], axis))


def cube_swap(buffer, axis, index, name, distance=1):
    sent = pick(buffer, axis, 1 - index)
    received = across(sent.reshape(-1, sent.shape[-1]), name, distance).reshape(sent.shape)
    return ordered(pick(buffer, axis, index), received, axis, index)


def normalise(rows):
    mean = jnp.mean(rows, axis=-1, keepdims=True)
    centred = rows - mean
    variance = jnp.mean(centred * centred, axis=-1, keepdims=True)
    inverse = lax.rsqrt(variance + EPS)
    return centred * inverse, inverse


def column_block(codes, weight, rows, grads):
    own_feats, _, width = rows.shape
    pre = jnp.dot(codes, weight, preferred_element_type=jnp.float32)
    normed, grad_pre = [], []
    for f in range(own_feats):
        v = pre[:, f * width : (f + 1) * width]
        sigma = jax.nn.sigmoid(v)
        fmb = (v * sigma).astype(jnp.bfloat16).astype(jnp.float32)
        y, inverse = normalise(fmb + rows[f].astype(jnp.float32))
        g = grads[f].astype(jnp.float32)
        mean_g = jnp.mean(g, axis=-1, keepdims=True)
        mean_gy = jnp.mean(g * y, axis=-1, keepdims=True)
        grad_fmb = (inverse * (g - mean_g - y * mean_gy)).astype(jnp.bfloat16).astype(jnp.float32)
        normed.append(y.astype(jnp.bfloat16))
        grad_pre.append((grad_fmb * (sigma * (1.0 + v * (1.0 - sigma)))).astype(jnp.bfloat16))
    return jnp.stack(normed), jnp.concatenate(grad_pre, axis=1)


def shards(panels, cotangent, fm_proj, mlp_weight, compress_weight):
    blocks = lax.axis_size(BATCH)
    owners = lax.axis_size(MP)
    peers = owners // 2
    lines = lax.axis_size("x")
    core, far, x = (lax.axis_index(name) for name in ("core", "far", "x"))
    group, feats_dev, width = panels.shape[1:]
    samples = group // blocks
    feats = feats_dev * blocks
    rank = fm_proj.shape[1]
    own_feats = NF // owners
    half = peers * samples
    code_cols = feats * rank
    code_blocks = code_cols // width
    lanes = width // 2

    def x_swap(buffer, step):
        distance = 1 << step
        split = buffer.reshape(lines // distance // 2, 2, distance, *buffer.shape[1:])
        return cube_swap(split, 1, (x >> step) & 1, "x", distance).reshape(buffer.shape)

    def by_owner(rows):
        rows = rows.reshape(samples, owners, own_feats, width).transpose(1, 2, 0, 3)
        return rows.reshape(lines, 2, 2, own_feats, samples, width)

    steps = range(lines.bit_length() - 1)
    head_grads = by_owner(cotangent[0, :, :NF])
    for step in steps:
        head_grads = x_swap(head_grads, step)

    owned = swap(panels.reshape(blocks, samples, feats_dev, width), BATCH)
    owned = after(owned, head_grads)
    wide = owned.transpose(1, 0, 2, 3).reshape(samples, feats, width)
    inner = jnp.einsum("snd,nk->sdk", wide, fm_proj, preferred_element_type=jnp.float32)
    codes = jnp.einsum(
        "snd,sdk->snk", wide.astype(jnp.float32), inner, precision=lax.Precision.HIGHEST
    )
    codes = codes.astype(jnp.bfloat16).reshape(samples, code_blocks, width).transpose(1, 0, 2)

    code_rows = code_blocks * samples
    head_rows = own_feats * samples
    heads = by_owner(wide[:, :NF]).reshape(peers, 2, head_rows, width)
    heads = jnp.where(core == 0, heads, heads[:, ::-1]).reshape(peers, 2 * head_rows, width)
    parcel = jnp.broadcast_to(codes.reshape(-1, width), (peers, code_rows, width))
    parcel = jnp.concatenate([parcel, heads], axis=1)
    head_grads = cube_swap(after(head_grads, parcel), 2, core, "core")
    head_grads = cube_swap(head_grads, 1, far, "far").reshape(peers, 2, head_rows, width)
    parcel_mine = after(swap(parcel, ("x", "far")), head_grads)
    parcel_other = across(parcel_mine.reshape(-1, width), "core").reshape(parcel_mine.shape)
    mine, other = (
        p[:, :code_rows].reshape(peers, code_blocks, samples, width)
        for p in (parcel_mine, parcel_other)
    )

    def tall(rows):
        rows = rows.reshape(2 * peers, own_feats, samples, width).transpose(1, 0, 2, 3)
        return rows.reshape(own_feats, 2 * half, width)

    near_blocks = code_blocks // 2
    left_mine = mine.reshape(peers, code_blocks // 4, 2, 2, samples, 2, lanes)
    left_mine = left_mine.transpose(2, 5, 0, 1, 3, 4, 6).reshape(4, -1, lanes)
    left_mine = swap(left_mine, ("yl", "twin"))
    left_other = across(left_mine.reshape(-1, lanes), "core")

    def columns(left):
        left = left.reshape(4 * peers, near_blocks, samples, lanes).transpose(0, 2, 1, 3)
        return left.reshape(4 * half, near_blocks * lanes)

    both = jnp.concatenate([mine, other]).transpose(0, 2, 1, 3).reshape(2 * half, code_cols)
    rows = jnp.concatenate(
        [parcel_mine[:, code_rows : code_rows + head_rows], parcel_other[:, code_rows + head_rows :]]
    )
    grads = jnp.concatenate([pick(head_grads, 1, core), pick(head_grads, 1, 1 - core)])
    normed, grad_pre = column_block(both, mlp_weight, tall(rows), tall(grads))
    near_grads = jnp.broadcast_to(grad_pre, (4, *grad_pre.shape))
    near_grads = after(near_grads, left_mine)
    back = after(normed, near_grads)
    near_grads = swap(near_grads, ("yl", "twin")).reshape(4, 2, half, -1)

    def product(left, right):
        right = right.reshape(4 * half, -1)
        return jnp.einsum("sc,so->co", columns(left), right, preferred_element_type=jnp.float32)

    term = product(left_mine, near_grads[:, 0]) + product(left_other, near_grads[:, 1])
    term = term.astype(jnp.bfloat16).reshape(code_blocks // 2, lanes, -1)
    mlp_grad = jnp.sum(swap(term, ("yh", "pair")).astype(jnp.float32), axis=0)

    back = back.reshape(own_feats, 2, lines, 2, samples, width).transpose(1, 0, 2, 3, 4, 5)
    back = ordered(back[0], back[1], 0, core).transpose(2, 3, 0, 1, 4, 5)
    back = cube_swap(back, 2, core, "core")
    back = cube_swap(back, 1, far, "far")
    back = after(back, term)
    for step in steps:
        back = x_swap(back, step)
    head = back.transpose(4, 0, 1, 2, 3, 5).reshape(samples, NF, width)

    lcb = jnp.einsum("pm,qmo->qpo", compress_weight, wide, preferred_element_type=jnp.float32)
    tail, _ = normalise(lcb + wide[:, NF:].astype(jnp.float32))
    result = jnp.concatenate([head, tail.astype(jnp.bfloat16)], axis=1)
    return result[None], mlp_grad


def solution(mesh):
    fine = Mesh(mesh.devices.reshape([n for _, n in FINE]), [name for name, _ in FINE])
    in_specs = (P(MP, None, BATCH, None), P(MP, BATCH, None, None), P(), P(None, MP), P())
    out_specs = (P(MP, BATCH, None, None), P(BATCH, MP))
    return jax.shard_map(shards, mesh=fine, in_specs=in_specs, out_specs=out_specs, check_vma=False)
```

```python
import jax
import jax.numpy as jnp
from jax import lax
from jax.sharding import Mesh
from jax.sharding import PartitionSpec as P

NF = 64
EPS = 1e-05
FINE = (("yh", 4), ("yl", 2), ("pair", 2), ("twin", 2), ("x", 8), ("far", 2), ("core", 2))
BATCH = ("yh", "yl", "pair", "twin")
MP = ("x", "far", "core")


def swap(chunks, axes):
    return lax.all_to_all(chunks, axes, split_axis=0, concat_axis=0, tiled=True)


def across(array, axis, distance=1):
    count = lax.axis_size(axis)
    return lax.ppermute(array, axis, [(i, i ^ distance) for i in range(count)])


def after(array, *others):
    return lax.optimization_barrier((array, *others))[0]


def pick(array, axis, index):
    return jnp.where(
        index == 0, lax.index_in_dim(array, 0, axis, False), lax.index_in_dim(array, 1, axis, False)
    )


def ordered(own, other, axis, index):
    return jnp.where(index == 0, jnp.stack([own, other], axis), jnp.stack([other, own], axis))


def cube_swap(buffer, axis, index, name, distance=1):
    sent = pick(buffer, axis, 1 - index)
    received = across(sent.reshape(-1, sent.shape[-1]), name, distance).reshape(sent.shape)
    return ordered(pick(buffer, axis, index), received, axis, index)


def two_bits(buffer, x):
    def relative(entries):
        low, high = x & 1 == 0, x & 2 == 0
        return [
            jnp.where(
                high,
                jnp.where(low, entries[d], entries[1 ^ d]),
                jnp.where(low, entries[2 ^ d], entries[3 ^ d]),
            )
            for d in range(4)
        ]

    buffer = buffer.reshape(2, 4, *buffer.shape[1:])
    entries = relative([buffer[:, i] for i in range(4)])
    flat = [entry.reshape(-1, entry.shape[-1]) for entry in entries]
    moved = [flat[0]] + [across(flat[d], "x", d) for d in (1, 2, 3)]
    moved = relative([entry.reshape(entries[0].shape) for entry in moved])
    return jnp.stack(moved, axis=1).reshape(-1, *buffer.shape[2:])


def normalise(rows):
    mean = jnp.mean(rows, axis=-1, keepdims=True)
    centred = rows - mean
    variance = jnp.mean(centred * centred, axis=-1, keepdims=True)
    inverse = lax.rsqrt(variance + EPS)
    return centred * inverse, inverse


def column_block(codes, weight, rows, grads):
    own_feats, _, width = rows.shape
    pre = jnp.dot(codes, weight, preferred_element_type=jnp.float32)
    normed, grad_pre = [], []
    for f in range(own_feats):
        v = pre[:, f * width : (f + 1) * width]
        sigma = jax.nn.sigmoid(v)
        fmb = (v * sigma).astype(jnp.bfloat16).astype(jnp.float32)
        y, inverse = normalise(fmb + rows[f].astype(jnp.float32))
        g = grads[f].astype(jnp.float32)
        mean_g = jnp.mean(g, axis=-1, keepdims=True)
        mean_gy = jnp.mean(g * y, axis=-1, keepdims=True)
        grad_fmb = (inverse * (g - mean_g - y * mean_gy)).astype(jnp.bfloat16).astype(jnp.float32)
        normed.append(y.astype(jnp.bfloat16))
        grad_pre.append((grad_fmb * (sigma * (1.0 + v * (1.0 - sigma)))).astype(jnp.bfloat16))
    return jnp.stack(normed), jnp.concatenate(grad_pre, axis=1)


def shards(panels, cotangent, fm_proj, mlp_weight, compress_weight):
    blocks = lax.axis_size(BATCH)
    owners = lax.axis_size(MP)
    peers = owners // 2
    lines = lax.axis_size("x")
    core, far, x, yl, twin = (lax.axis_index(name) for name in ("core", "far", "x", "yl", "twin"))
    group, feats_dev, width = panels.shape[1:]
    samples = group // blocks
    feats = feats_dev * blocks
    rank = fm_proj.shape[1]
    own_feats = NF // owners
    half = peers * samples
    code_cols = feats * rank
    code_blocks = code_cols // width
    lanes = width // 2

    def x_swap(buffer, step):
        distance = 1 << step
        split = buffer.reshape(lines // distance // 2, 2, distance, *buffer.shape[1:])
        return cube_swap(split, 1, (x >> step) & 1, "x", distance).reshape(buffer.shape)

    def by_owner(rows):
        rows = rows.reshape(samples, owners, own_feats, width).transpose(1, 2, 0, 3)
        return rows.reshape(lines, 2, 2, own_feats, samples, width)

    steps = range(lines.bit_length() - 1)
    head_grads = by_owner(cotangent[0, :, :NF])
    for step in steps:
        head_grads = x_swap(head_grads, step)

    owned = swap(panels.reshape(blocks, samples, feats_dev, width), BATCH)
    owned = after(owned, head_grads)
    wide = owned.transpose(1, 0, 2, 3).reshape(samples, feats, width)
    inner = jnp.einsum("snd,nk->sdk", wide, fm_proj, preferred_element_type=jnp.float32)
    codes = jnp.einsum(
        "snd,sdk->snk", wide.astype(jnp.float32), inner, precision=lax.Precision.HIGHEST
    )
    codes = codes.astype(jnp.bfloat16).reshape(samples, code_blocks, width).transpose(1, 0, 2)

    code_rows = code_blocks * samples
    head_rows = own_feats * samples
    heads = by_owner(wide[:, :NF]).reshape(peers, 2, head_rows, width)
    heads = jnp.where(core == 0, heads, heads[:, ::-1]).reshape(peers, 2 * head_rows, width)
    parcel = jnp.broadcast_to(codes.reshape(-1, width), (peers, code_rows, width))
    parcel = jnp.concatenate([parcel, heads], axis=1)
    head_grads = cube_swap(after(head_grads, parcel), 2, core, "core")
    head_grads = cube_swap(head_grads, 1, far, "far").reshape(peers, 2, head_rows, width)
    parcel_mine = after(swap(parcel, ("x", "far")), head_grads)
    parcel_other = across(parcel_mine.reshape(-1, width), "core").reshape(parcel_mine.shape)
    mine, other = (
        p[:, :code_rows].reshape(peers, code_blocks, samples, width)
        for p in (parcel_mine, parcel_other)
    )

    def tall(rows):
        rows = rows.reshape(2 * peers, own_feats, samples, width).transpose(1, 0, 2, 3)
        return rows.reshape(own_feats, 2 * half, width)

    near_blocks = code_blocks // 2
    left_mine = mine.reshape(peers, code_blocks // 4, 2, 2, samples, 2, lanes)
    left_mine = left_mine.transpose(2, 5, 0, 1, 3, 4, 6).reshape(4, -1, lanes)
    left_mine = swap(left_mine, ("yl", "twin"))

    def columns(left):
        left = left.reshape(4 * peers, near_blocks, samples, lanes).transpose(0, 2, 1, 3)
        return left.reshape(4 * half, near_blocks * lanes)

    both = jnp.concatenate([mine, other]).transpose(0, 2, 1, 3).reshape(2 * half, code_cols)
    rows = jnp.concatenate(
        [parcel_mine[:, code_rows : code_rows + head_rows], parcel_other[:, code_rows + head_rows :]]
    )
    grads = jnp.concatenate([pick(head_grads, 1, core), pick(head_grads, 1, 1 - core)])
    normed, grad_pre = column_block(both, mlp_weight, tall(rows), tall(grads))
    near_own = across(grad_pre, "yl")
    twin_grads = across(grad_pre, "twin")
    near_twin = across(twin_grads, "yl")
    left_other = across(after(left_mine, grad_pre).reshape(-1, lanes), "core")
    back = after(normed, grad_pre)

    def halves_of(index):
        here = jnp.where(twin == index % 2, grad_pre, twin_grads)
        there = jnp.where(twin == index % 2, near_own, near_twin)
        return jnp.where(yl == index // 2, here, there).reshape(2, half, -1)

    grads = [halves_of(index) for index in range(4)]

    def product(left, right):
        right = jnp.concatenate(right, axis=0)
        return jnp.einsum("sc,so->co", columns(left), right, preferred_element_type=jnp.float32)

    term = product(left_mine, [g[0] for g in grads]) + product(left_other, [g[1] for g in grads])
    term = term.astype(jnp.bfloat16).reshape(code_blocks // 2, lanes, -1)
    back = back.reshape(own_feats, 2, lines, 2, samples, width).transpose(1, 0, 2, 3, 4, 5)
    back = ordered(back[0], back[1], 0, core).transpose(2, 3, 0, 1, 4, 5)
    back = cube_swap(back, 2, core, "core")
    back = cube_swap(back, 1, far, "far")
    back = after(back, term)
    mlp_grad = jnp.sum(swap(term, ("yh", "pair")).astype(jnp.float32), axis=0)
    if lines == 8:
        back = two_bits(back, x)
    for step in steps[2 if lines == 8 else 0 :]:
        back = x_swap(back, step)
    head = back.transpose(4, 0, 1, 2, 3, 5).reshape(samples, NF, width)

    lcb = jnp.einsum("pm,qmo->qpo", compress_weight, wide, preferred_element_type=jnp.float32)
    tail, _ = normalise(lcb + wide[:, NF:].astype(jnp.float32))
    result = jnp.concatenate([head, tail.astype(jnp.bfloat16)], axis=1)
    return result[None], mlp_grad


def solution(mesh):
    fine = Mesh(mesh.devices.reshape([n for _, n in FINE]), [name for name, _ in FINE])
    in_specs = (P(MP, None, BATCH, None), P(MP, BATCH, None, None), P(), P(None, MP), P())
    out_specs = (P(MP, BATCH, None, None), P(BATCH, MP))
    return jax.shard_map(shards, mesh=fine, in_specs=in_specs, out_specs=out_specs, check_vma=False)
```

```python
import jax
import jax.numpy as jnp
from jax import lax
from jax.sharding import Mesh
from jax.sharding import PartitionSpec as P

NF = 64
EPS = 1e-05
FINE = (("yh", 4), ("yl", 2), ("pair", 2), ("twin", 2), ("x", 8), ("far", 2), ("core", 2))
BATCH = ("yh", "yl", "pair", "twin")
MP = ("x", "far", "core")


def swap(chunks, axes):
    return lax.all_to_all(chunks, axes, split_axis=0, concat_axis=0, tiled=True)


def across(array, axis, distance=1):
    count = lax.axis_size(axis)
    return lax.ppermute(array, axis, [(i, i ^ distance) for i in range(count)])


def after(array, *others):
    return lax.optimization_barrier((array, *others))[0]


def pick(array, axis, index):
    return jnp.where(
        index == 0, lax.index_in_dim(array, 0, axis, False), lax.index_in_dim(array, 1, axis, False)
    )


def ordered(own, other, axis, index):
    return jnp.where(index == 0, jnp.stack([own, other], axis), jnp.stack([other, own], axis))


def cube_swap(buffer, axis, index, name, distance=1):
    sent = pick(buffer, axis, 1 - index)
    received = across(sent.reshape(-1, sent.shape[-1]), name, distance).reshape(sent.shape)
    return ordered(pick(buffer, axis, index), received, axis, index)


def two_bits(buffer, x):
    def relative(entries):
        low, high = x & 1 == 0, x & 2 == 0
        return [
            jnp.where(
                high,
                jnp.where(low, entries[d], entries[1 ^ d]),
                jnp.where(low, entries[2 ^ d], entries[3 ^ d]),
            )
            for d in range(4)
        ]

    buffer = buffer.reshape(2, 4, *buffer.shape[1:])
    entries = relative([buffer[:, i] for i in range(4)])
    flat = [entry.reshape(-1, entry.shape[-1]) for entry in entries]
    moved = [flat[0]] + [across(flat[d], "x", d) for d in (1, 2, 3)]
    moved = relative([entry.reshape(entries[0].shape) for entry in moved])
    return jnp.stack(moved, axis=1).reshape(-1, *buffer.shape[2:])


def normalise(rows):
    mean = jnp.mean(rows, axis=-1, keepdims=True)
    centred = rows - mean
    variance = jnp.mean(centred * centred, axis=-1, keepdims=True)
    inverse = lax.rsqrt(variance + EPS)
    return centred * inverse, inverse


def column_block(codes, weight, rows, grads):
    own_feats, _, width = rows.shape
    pre = jnp.dot(codes, weight, preferred_element_type=jnp.float32)
    normed, grad_pre = [], []
    for f in range(own_feats):
        v = pre[:, f * width : (f + 1) * width]
        sigma = jax.nn.sigmoid(v)
        fmb = (v * sigma).astype(jnp.bfloat16).astype(jnp.float32)
        y, inverse = normalise(fmb + rows[f].astype(jnp.float32))
        g = grads[f].astype(jnp.float32)
        mean_g = jnp.mean(g, axis=-1, keepdims=True)
        mean_gy = jnp.mean(g * y, axis=-1, keepdims=True)
        grad_fmb = (inverse * (g - mean_g - y * mean_gy)).astype(jnp.bfloat16).astype(jnp.float32)
        normed.append(y.astype(jnp.bfloat16))
        grad_pre.append((grad_fmb * (sigma * (1.0 + v * (1.0 - sigma)))).astype(jnp.bfloat16))
    return jnp.stack(normed), jnp.concatenate(grad_pre, axis=1)


def shards(panels, cotangent, fm_proj, mlp_weight, compress_weight):
    blocks = lax.axis_size(BATCH)
    owners = lax.axis_size(MP)
    peers = owners // 2
    lines = lax.axis_size("x")
    core, far, x, yl, twin = (lax.axis_index(name) for name in ("core", "far", "x", "yl", "twin"))
    group, feats_dev, width = panels.shape[1:]
    samples = group // blocks
    feats = feats_dev * blocks
    rank = fm_proj.shape[1]
    own_feats = NF // owners
    half = peers * samples
    code_cols = feats * rank
    code_blocks = code_cols // width
    lanes = width // 2

    def x_swap(buffer, step):
        distance = 1 << step
        split = buffer.reshape(lines // distance // 2, 2, distance, *buffer.shape[1:])
        return cube_swap(split, 1, (x >> step) & 1, "x", distance).reshape(buffer.shape)

    def by_owner(rows):
        rows = rows.reshape(samples, owners, own_feats, width).transpose(1, 2, 0, 3)
        return rows.reshape(lines, 2, 2, own_feats, samples, width)

    steps = range(lines.bit_length() - 1)
    head_grads = by_owner(cotangent[0, :, :NF])
    for step in steps:
        head_grads = x_swap(head_grads, step)

    owned = swap(panels.reshape(blocks, samples, feats_dev, width), BATCH)
    owned = after(owned, head_grads)
    wide = owned.transpose(1, 0, 2, 3).reshape(samples, feats, width)
    inner = jnp.einsum("snd,nk->sdk", wide, fm_proj, preferred_element_type=jnp.float32)
    codes = jnp.einsum(
        "snd,sdk->snk", wide.astype(jnp.float32), inner, precision=lax.Precision.HIGHEST
    )
    codes = codes.astype(jnp.bfloat16).reshape(samples, code_blocks, width).transpose(1, 0, 2)

    code_rows = code_blocks * samples
    head_rows = own_feats * samples
    heads = by_owner(wide[:, :NF]).reshape(peers, 2, head_rows, width)
    heads = jnp.where(core == 0, heads, heads[:, ::-1]).reshape(peers, 2 * head_rows, width)
    parcel = jnp.broadcast_to(codes.reshape(-1, width), (peers, code_rows, width))
    parcel = jnp.concatenate([parcel, heads], axis=1)
    head_grads = cube_swap(after(head_grads, parcel), 2, core, "core")
    head_grads = cube_swap(head_grads, 1, far, "far").reshape(peers, 2, head_rows, width)
    parcel_mine = after(swap(parcel, ("x", "far")), head_grads)
    parcel_other = across(parcel_mine.reshape(-1, width), "core").reshape(parcel_mine.shape)
    mine, other = (
        p[:, :code_rows].reshape(peers, code_blocks, samples, width)
        for p in (parcel_mine, parcel_other)
    )

    def tall(rows):
        rows = rows.reshape(2 * peers, own_feats, samples, width).transpose(1, 0, 2, 3)
        return rows.reshape(own_feats, 2 * half, width)

    near_blocks = code_blocks // 2
    left_mine = mine.reshape(peers, code_blocks // 4, 2, 2, samples, 2, lanes)
    left_mine = left_mine.transpose(2, 5, 0, 1, 3, 4, 6).reshape(4, -1, lanes)
    left_mine = swap(left_mine, ("yl", "twin"))

    def columns(left):
        left = left.reshape(4 * peers, near_blocks, samples, lanes).transpose(0, 2, 1, 3)
        return left.reshape(4 * half, near_blocks * lanes)

    both = jnp.concatenate([mine, other]).transpose(0, 2, 1, 3).reshape(2 * half, code_cols)
    rows = jnp.concatenate(
        [parcel_mine[:, code_rows : code_rows + head_rows], parcel_other[:, code_rows + head_rows :]]
    )
    grads = jnp.concatenate([pick(head_grads, 1, core), pick(head_grads, 1, 1 - core)])
    normed, grad_pre = column_block(both, mlp_weight, tall(rows), tall(grads))
    near_twin = across(grad_pre, ("yl", "twin"), 3)
    twin_grads = across(grad_pre, "twin")
    near_own = across(grad_pre, "yl")
    left_other = across(after(left_mine, grad_pre).reshape(-1, lanes), "core")
    back = after(normed, grad_pre)

    def halves_of(index):
        here = jnp.where(twin == index % 2, grad_pre, twin_grads)
        there = jnp.where(twin == index % 2, near_own, near_twin)
        return jnp.where(yl == index // 2, here, there).reshape(2, half, -1)

    grads = [halves_of(index) for index in range(4)]

    def product(left, right):
        right = jnp.concatenate(right, axis=0)
        return jnp.einsum("sc,so->co", columns(left), right, preferred_element_type=jnp.float32)

    term = product(left_mine, [g[0] for g in grads]) + product(left_other, [g[1] for g in grads])
    term = term.astype(jnp.bfloat16).reshape(code_blocks // 2, lanes, -1)
    back = back.reshape(own_feats, 2, lines, 2, samples, width).transpose(1, 0, 2, 3, 4, 5)
    back = ordered(back[0], back[1], 0, core).transpose(2, 3, 0, 1, 4, 5)
    back = cube_swap(back, 2, core, "core")
    back = cube_swap(back, 1, far, "far")
    back = after(back, term)
    mlp_grad = jnp.sum(swap(term, ("yh", "pair")).astype(jnp.float32), axis=0)
    if lines == 8:
        back = two_bits(back, x)
    for step in steps[2 if lines == 8 else 0 :]:
        back = x_swap(back, step)
    head = back.transpose(4, 0, 1, 2, 3, 5).reshape(samples, NF, width)

    lcb = jnp.einsum("pm,qmo->qpo", compress_weight, wide, preferred_element_type=jnp.float32)
    tail, _ = normalise(lcb + wide[:, NF:].astype(jnp.float32))
    result = jnp.concatenate([head, tail.astype(jnp.bfloat16)], axis=1)
    return result[None], mlp_grad


def solution(mesh):
    fine = Mesh(mesh.devices.reshape([n for _, n in FINE]), [name for name, _ in FINE])
    in_specs = (P(MP, None, BATCH, None), P(MP, BATCH, None, None), P(), P(None, MP), P())
    out_specs = (P(MP, BATCH, None, None), P(BATCH, MP))
    return jax.shard_map(shards, mesh=fine, in_specs=in_specs, out_specs=out_specs, check_vma=False)
```

```python
import jax
import jax.numpy as jnp
from jax import lax
from jax.sharding import Mesh
from jax.sharding import PartitionSpec as P

NF = 64
EPS = 1e-05
FINE = (("yh", 4), ("yl", 2), ("pair", 2), ("twin", 2), ("x", 8), ("far", 2), ("core", 2))
BATCH = ("yh", "yl", "pair", "twin")
MP = ("x", "far", "core")


def swap(chunks, axes):
    return lax.all_to_all(chunks, axes, split_axis=0, concat_axis=0, tiled=True)


def across(array, axis, distance=1):
    count = lax.axis_size(axis)
    return lax.ppermute(array, axis, [(i, i ^ distance) for i in range(count)])


def after(array, *others):
    return lax.optimization_barrier((array, *others))[0]


def pick(array, axis, index):
    return jnp.where(
        index == 0, lax.index_in_dim(array, 0, axis, False), lax.index_in_dim(array, 1, axis, False)
    )


def ordered(own, other, axis, index):
    return jnp.where(index == 0, jnp.stack([own, other], axis), jnp.stack([other, own], axis))


def cube_swap(buffer, axis, index, name, distance=1):
    sent = pick(buffer, axis, 1 - index)
    received = across(sent.reshape(-1, sent.shape[-1]), name, distance).reshape(sent.shape)
    return ordered(pick(buffer, axis, index), received, axis, index)


def two_bits(buffer, x):
    def relative(entries):
        low, high = x & 1 == 0, x & 2 == 0
        return [
            jnp.where(
                high,
                jnp.where(low, entries[d], entries[1 ^ d]),
                jnp.where(low, entries[2 ^ d], entries[3 ^ d]),
            )
            for d in range(4)
        ]

    buffer = buffer.reshape(2, 4, *buffer.shape[1:])
    entries = relative([buffer[:, i] for i in range(4)])
    flat = [entry.reshape(-1, entry.shape[-1]) for entry in entries]
    moved = [flat[0]] + [across(flat[d], "x", d) for d in (1, 2, 3)]
    moved = relative([entry.reshape(entries[0].shape) for entry in moved])
    return jnp.stack(moved, axis=1).reshape(-1, *buffer.shape[2:])


def normalise(rows):
    mean = jnp.mean(rows, axis=-1, keepdims=True)
    centred = rows - mean
    variance = jnp.mean(centred * centred, axis=-1, keepdims=True)
    inverse = lax.rsqrt(variance + EPS)
    return centred * inverse, inverse


def column_block(codes, weight, rows, grads):
    own_feats, _, width = rows.shape
    pre = jnp.dot(codes, weight, preferred_element_type=jnp.float32)
    normed, grad_pre = [], []
    for f in range(own_feats):
        v = pre[:, f * width : (f + 1) * width]
        sigma = jax.nn.sigmoid(v)
        fmb = (v * sigma).astype(jnp.bfloat16).astype(jnp.float32)
        y, inverse = normalise(fmb + rows[f].astype(jnp.float32))
        g = grads[f].astype(jnp.float32)
        mean_g = jnp.mean(g, axis=-1, keepdims=True)
        mean_gy = jnp.mean(g * y, axis=-1, keepdims=True)
        grad_fmb = (inverse * (g - mean_g - y * mean_gy)).astype(jnp.bfloat16).astype(jnp.float32)
        normed.append(y.astype(jnp.bfloat16))
        grad_pre.append((grad_fmb * (sigma * (1.0 + v * (1.0 - sigma)))).astype(jnp.bfloat16))
    return jnp.stack(normed), jnp.concatenate(grad_pre, axis=1)


def shards(panels, cotangent, fm_proj, mlp_weight, compress_weight):
    blocks = lax.axis_size(BATCH)
    owners = lax.axis_size(MP)
    peers = owners // 2
    lines = lax.axis_size("x")
    core, far, x, yl, twin = (lax.axis_index(name) for name in ("core", "far", "x", "yl", "twin"))
    group, feats_dev, width = panels.shape[1:]
    samples = group // blocks
    feats = feats_dev * blocks
    rank = fm_proj.shape[1]
    own_feats = NF // owners
    half = peers * samples
    code_cols = feats * rank
    code_blocks = code_cols // width
    lanes = width // 2

    def x_swap(buffer, step):
        distance = 1 << step
        split = buffer.reshape(lines // distance // 2, 2, distance, *buffer.shape[1:])
        return cube_swap(split, 1, (x >> step) & 1, "x", distance).reshape(buffer.shape)

    def by_owner(rows):
        rows = rows.reshape(samples, owners, own_feats, width).transpose(1, 2, 0, 3)
        return rows.reshape(lines, 2, 2, own_feats, samples, width)

    steps = range(lines.bit_length() - 1)
    head_grads = by_owner(cotangent[0, :, :NF])
    for step in steps:
        head_grads = x_swap(head_grads, step)

    owned = swap(panels.reshape(blocks, samples, feats_dev, width), BATCH)
    owned = after(owned, head_grads)
    wide = owned.transpose(1, 0, 2, 3).reshape(samples, feats, width)
    inner = jnp.einsum("snd,nk->sdk", wide, fm_proj, preferred_element_type=jnp.float32)
    codes = jnp.einsum(
        "snd,sdk->snk", wide.astype(jnp.float32), inner, precision=lax.Precision.HIGHEST
    )
    codes = codes.astype(jnp.bfloat16).reshape(samples, code_blocks, width).transpose(1, 0, 2)

    code_rows = code_blocks * samples
    head_rows = own_feats * samples
    heads = by_owner(wide[:, :NF]).reshape(peers, 2, head_rows, width)
    heads = jnp.where(core == 0, heads, heads[:, ::-1]).reshape(peers, 2 * head_rows, width)
    parcel = jnp.broadcast_to(codes.reshape(-1, width), (peers, code_rows, width))
    parcel = jnp.concatenate([parcel, heads], axis=1)
    head_grads = cube_swap(after(head_grads, parcel), 2, core, "core")
    head_grads = cube_swap(head_grads, 1, far, "far").reshape(peers, 2, head_rows, width)
    parcel_mine = after(swap(parcel, ("x", "far")), head_grads)
    parcel_other = across(parcel_mine.reshape(-1, width), "core").reshape(parcel_mine.shape)
    mine, other = (
        p[:, :code_rows].reshape(peers, code_blocks, samples, width)
        for p in (parcel_mine, parcel_other)
    )

    def tall(rows):
        rows = rows.reshape(2 * peers, own_feats, samples, width).transpose(1, 0, 2, 3)
        return rows.reshape(own_feats, 2 * half, width)

    near_blocks = code_blocks // 2
    left_mine = mine.reshape(peers, code_blocks // 4, 2, 2, samples, 2, lanes)
    left_mine = left_mine.transpose(2, 5, 0, 1, 3, 4, 6).reshape(4, -1, lanes)
    left_mine = swap(left_mine, ("yl", "twin"))

    def columns(left):
        left = left.reshape(4 * peers, near_blocks, samples, lanes).transpose(0, 2, 1, 3)
        return left.reshape(4 * half, near_blocks * lanes)

    both = jnp.concatenate([mine, other]).transpose(0, 2, 1, 3).reshape(2 * half, code_cols)
    rows = jnp.concatenate(
        [parcel_mine[:, code_rows : code_rows + head_rows], parcel_other[:, code_rows + head_rows :]]
    )
    grads = jnp.concatenate([pick(head_grads, 1, core), pick(head_grads, 1, 1 - core)])
    normed, grad_pre = column_block(both, mlp_weight, tall(rows), tall(grads))
    near_own = across(grad_pre, "yl")
    twin_grads = across(grad_pre, "twin")
    near_twin = across(twin_grads, "yl")
    left_other = across(after(left_mine, grad_pre).reshape(-1, lanes), "core")
    back = after(normed, grad_pre)

    def halves_of(index):
        here = jnp.where(twin == index % 2, grad_pre, twin_grads)
        there = jnp.where(twin == index % 2, near_own, near_twin)
        return jnp.where(yl == index // 2, here, there).reshape(2, half, -1)

    grads = [halves_of(index) for index in range(4)]

    def product(left, right):
        right = jnp.concatenate(right, axis=0)
        return jnp.einsum("sc,so->co", columns(left), right, preferred_element_type=jnp.float32)

    term = product(left_mine, [g[0] for g in grads]) + product(left_other, [g[1] for g in grads])
    term = term.astype(jnp.bfloat16).reshape(code_blocks // 2, lanes, -1)
    back = back.reshape(own_feats, 2, lines, 2, samples, width).transpose(1, 0, 2, 3, 4, 5)
    back = ordered(back[0], back[1], 0, core).transpose(2, 3, 0, 1, 4, 5)
    back = cube_swap(back, 2, core, "core")
    back = cube_swap(back, 1, far, "far")
    if lines == 8:
        back = x_swap(back, 2)
    back = after(back, term)
    mlp_grad = jnp.sum(swap(term, ("yh", "pair")).astype(jnp.float32), axis=0)
    if lines == 8:
        back = two_bits(back, x)
    for step in steps[3 if lines == 8 else 0 :]:
        back = x_swap(back, step)
    head = back.transpose(4, 0, 1, 2, 3, 5).reshape(samples, NF, width)

    lcb = jnp.einsum("pm,qmo->qpo", compress_weight, wide, preferred_element_type=jnp.float32)
    tail, _ = normalise(lcb + wide[:, NF:].astype(jnp.float32))
    result = jnp.concatenate([head, tail.astype(jnp.bfloat16)], axis=1)
    return result[None], mlp_grad


def solution(mesh):
    fine = Mesh(mesh.devices.reshape([n for _, n in FINE]), [name for name, _ in FINE])
    in_specs = (P(MP, None, BATCH, None), P(MP, BATCH, None, None), P(), P(None, MP), P())
    out_specs = (P(MP, BATCH, None, None), P(BATCH, MP))
    return jax.shard_map(shards, mesh=fine, in_specs=in_specs, out_specs=out_specs, check_vma=False)
```
